32 devices in a mesh: grp: 2 (over y), wt: 4 (over x, core), tm: 4 (over z).
Axes of the slice: x: 2, y: 2, z: 4, core: 2. Of those that a mesh axis runs over, the one named last changes fastest.
Arguments:
- signal: bfloat16 [5120, 512], P(('grp', 'tm')), parts along dimension 0, may hold values from -6 to 6
- cotangent: bfloat16 [5120, 512], P(('grp', 'tm')), parts along dimension 0, may hold values from -6 to 6
- first_filter_taps: bfloat16 [3, 512, 1024], P(None, None, 'wt'), may hold values from -0.15625 to 0.15625
- first_gate_taps: bfloat16 [3, 512, 1024], P(None, None, 'wt'), may hold values from -0.15625 to 0.15625
- first_residual_projection: bfloat16 [1024, 512], P('wt'), may hold values from -0.1875 to 0.1875
- second_filter_taps: bfloat16 [3, 512, 1024], P(None, None, 'wt'), may hold values from -0.15625 to 0.15625
- second_gate_taps: bfloat16 [3, 512, 1024], P(None, None, 'wt'), may hold values from -0.15625 to 0.15625
- second_residual_projection: bfloat16 [1024, 512], P('wt'), may hold values from -0.1875 to 0.1875
Outputs:
- second_layer_output: bfloat16 [5120, 512], P(('grp', 'tm', 'wt')), parts along dimension 0
- input_feature_gradient: bfloat16 [5120, 512], P(('grp', 'tm')), parts along dimension 0
- grad_filter_first: float32 [6, 512, 1024], P('grp', 'tm', 'wt'), parts along dimension 0
- grad_gate_first: float32 [6, 512, 1024], P('grp', 'tm', 'wt'), parts along dimension 0
- grad_mix_first: float32 [2048, 512], P(('grp', 'wt'), 'tm'), parts along dimension 0
- grad_filter_second: float32 [6, 512, 1024], P('grp', 'tm', 'wt'), parts along dimension 0
- grad_gate_second: float32 [6, 512, 1024], P('grp', 'tm', 'wt'), parts along dimension 0
- grad_mix_second: float32 [2048, 512], P(('grp', 'wt'), 'tm'), parts along dimension 0
The draws below stay inside these ranges and needn't reach their ends.
There are 2 independent parts, one for each index of `grp`. The reference program is written for one: setup_inputs(seed, part) draws one part's arguments, and reference() takes and returns one part's arrays. A program takes and returns all parts, laid end to end along the dimension named above; an argument that names none is the same for every part. Nothing has to cross between parts.
All inputs are finite; a program needn't handle non-finite values.
Results may differ from the reference program's by a relative error of at most 0.0065.
Values may be sent and summed in bfloat16 or wider, within the bound.
A program may use at most 64 MiB of HBM per device.

```python
import math
import jax
import jax.numpy as jnp
from jax import lax

C = 512
G = 1024
KW = 3
SEQ = 2560
FIRST_DILATION = 320
SECOND_DILATION = 640


def levels(rng, dims, pieces, low, largest):
    loudness = 1.0
    for position, blocks in pieces:
        heights = jax.random.uniform(jax.random.fold_in(jax.random.fold_in(rng, 6), position), (blocks,), jnp.float32, low / len(pieces), largest / len(pieces))
        loudness = loudness * jnp.repeat(jnp.exp(heights), dims[position] // blocks).reshape((-1,) + (1,) * (len(dims) - 1 - position))
    return loudness


def bell_draw(key, shape, deviation, reach, shards=(), held_as=jnp.bfloat16):
    result = jax.random.normal(key, shape, jnp.float32) * deviation
    if len(shards) > 0:
        result = levels(key, shape, shards, -0.22, 0.18) * result
    return jnp.clip(result, min=-reach, max=reach).astype(held_as)


def setup_inputs(seed: int = 0, part: int = 0) -> dict:
    streams_of = jax.random.split(jax.random.key(seed), 9)
    own_keys = jax.random.split(jax.random.fold_in(streams_of[8], part), 9)
    signal = bell_draw(own_keys[0], (SEQ, C), 1.0, 6.0, ((0, 4),))
    cotangent = bell_draw(own_keys[1], (SEQ, C), 1.0, 6.0, ((0, 4),))
    first_filter_taps = bell_draw(streams_of[2], (KW, C, G), (KW * C) ** -0.5, 0.15625, ((2, 4),))
    first_gate_taps = bell_draw(streams_of[3], (KW, C, G), (KW * C) ** -0.5, 0.15625, ((2, 4),))
    first_residual_projection = bell_draw(streams_of[4], (G, C), G ** -0.5, 0.1875, ((0, 4),))
    second_filter_taps = bell_draw(streams_of[5], (KW, C, G), (KW * C) ** -0.5, 0.15625, ((2, 4),))
    second_gate_taps = bell_draw(streams_of[6], (KW, C, G), (KW * C) ** -0.5, 0.15625, ((2, 4),))
    second_residual_projection = bell_draw(streams_of[7], (G, C), G ** -0.5, 0.1875, ((0, 4),))
    return {"signal": signal, "cotangent": cotangent, "first_filter_taps": first_filter_taps, "first_gate_taps": first_gate_taps, "first_residual_projection": first_residual_projection, "second_filter_taps": second_filter_taps, "second_gate_taps": second_gate_taps, "second_residual_projection": second_residual_projection}


def delayed(values, steps):
    return jnp.pad(values, ((steps, 0), (0, 0)))[:values.shape[0]]

def advanced(values, steps):
    return jnp.pad(values, ((0, steps), (0, 0)))[steps:]

def contract_rows(left_side, right_side):
    return lax.dot_general(left_side.astype(jnp.float32), right_side.astype(jnp.float32), (((0,), (0,)), ((), ())))

def contract_cols(left_side, right_side):
    return lax.dot_general(left_side.astype(jnp.float32), right_side.astype(jnp.float32), (((1,), (1,)), ((), ())))

def layer_forward_pass(signal, filter_weight, gate_weight, mix_weight, spread):
    joined = jnp.concatenate([filter_weight, gate_weight], axis=2)
    preact = jnp.zeros((signal.shape[0], joined.shape[2]), jnp.float32)
    for offset in range(KW):
        preact = preact + jnp.dot(delayed(signal, offset * spread), joined[offset], preferred_element_type=jnp.float32)
    tanh_part = jnp.tanh(preact[:, :G])
    sigmoid_part = jax.nn.sigmoid(preact[:, G:])
    gated = (tanh_part * sigmoid_part).astype(jnp.bfloat16)
    mixed = (signal.astype(jnp.float32) + jnp.dot(gated, mix_weight, preferred_element_type=jnp.float32)).astype(jnp.bfloat16)
    return (mixed, gated, tanh_part, sigmoid_part)

def layer_backward_pass(signal, filter_weight, gate_weight, mix_weight, spread, gated, tanh_part, sigmoid_part, upstream):
    joined = jnp.concatenate([filter_weight, gate_weight], axis=2)
    gated_grad = contract_cols(upstream, mix_weight)
    mix_grad = contract_rows(gated, upstream)
    filter_grad = gated_grad * sigmoid_part * (1.0 - tanh_part * tanh_part)
    gate_grad = gated_grad * tanh_part * sigmoid_part * (1.0 - sigmoid_part)
    preact_grad = jnp.concatenate([filter_grad, gate_grad], axis=1).astype(jnp.bfloat16)
    back_sum = jnp.zeros((signal.shape[0], signal.shape[1]), jnp.float32)
    conv_parts = []
    for offset in range(KW):
        later = advanced(preact_grad, offset * spread)
        back_sum = back_sum + contract_cols(later, joined[offset])
        conv_parts.append(contract_rows(signal, later))
    lowered = (upstream.astype(jnp.float32) + back_sum).astype(jnp.bfloat16)
    return (lowered, jnp.stack(conv_parts), mix_grad)

def reference(signal, cotangent, first_filter_taps, first_gate_taps, first_residual_projection, second_filter_taps, second_gate_taps, second_residual_projection):
    grad_scale = 1.0 / math.sqrt(SEQ)
    hidden_features, gated_output_first, tanh_branch_first, sigmoid_branch_first = layer_forward_pass(signal, first_filter_taps, first_gate_taps, first_residual_projection, FIRST_DILATION)
    second_layer_output, gated_output_second, tanh_branch_second, sigmoid_branch_second = layer_forward_pass(hidden_features, second_filter_taps, second_gate_taps, second_residual_projection, SECOND_DILATION)
    hidden_features_gradient, convolution_second_layer, projection_gradient_second = layer_backward_pass(hidden_features, second_filter_taps, second_gate_taps, second_residual_projection, SECOND_DILATION, gated_output_second, tanh_branch_second, sigmoid_branch_second, cotangent)
    input_feature_gradient, convolution_first_layer, projection_gradient_first = layer_backward_pass(signal, first_filter_taps, first_gate_taps, first_residual_projection, FIRST_DILATION, gated_output_first, tanh_branch_first, sigmoid_branch_first, hidden_features_gradient)
    return (second_layer_output, input_feature_gradient, convolution_first_layer[:, :, :G] * grad_scale, convolution_first_layer[:, :, G:] * grad_scale, projection_gradient_first * grad_scale, convolution_second_layer[:, :, :G] * grad_scale, convolution_second_layer[:, :, G:] * grad_scale, projection_gradient_second * grad_scale)
```

```python
import functools
import math

import jax
import jax.numpy as jnp
from jax import lax
from jax.experimental import pallas as pl
from jax.experimental.pallas import tpu as pltpu
from jax.sharding import PartitionSpec as P


def shifted(block, axis, distance):
    devices = range(lax.axis_size(axis))
    route = [(i - distance, i) for i in devices if i - distance in devices]
    return lax.ppermute(block, axis, route)


def contract_rows(left_side, right_side):
    return lax.dot_general(
        left_side, right_side, (((0,), (0,)), ((), ())), preferred_element_type=jnp.float32
    )


def contract_cols(left_side, right_side):
    return lax.dot_general(
        left_side, right_side, (((1,), (1,)), ((), ())), preferred_element_type=jnp.float32
    )


def apply_taps(tap_inputs, stacked):
    preact = jnp.dot(tap_inputs[0], stacked[0], preferred_element_type=jnp.float32)
    preact = preact + jnp.dot(tap_inputs[1], stacked[1], preferred_element_type=jnp.float32)
    return preact + jnp.dot(tap_inputs[2], stacked[2], preferred_element_type=jnp.float32)


def preact_short(signal, stacked):
    seg_rows = signal.shape[0]
    midpoint = seg_rows // 2
    earlier = shifted(signal, "tm", 1)
    joined = jnp.concatenate([earlier, signal], axis=0)
    tap_inputs = (signal, joined[midpoint : midpoint + seg_rows], earlier)
    return (apply_taps(tap_inputs, stacked), tap_inputs)


def preact_long(signal, stacked):
    one_back = shifted(signal, "tm", 1)
    two_back = shifted(signal, "tm", 2)
    tap_inputs = (signal, one_back, two_back)
    return (apply_taps(tap_inputs, stacked), tap_inputs)


def gate_units(preact, half_cols):
    tanh_part = jnp.tanh(preact[:, :half_cols])
    sigmoid_part = jax.nn.sigmoid(preact[:, half_cols:])
    return ((tanh_part * sigmoid_part).astype(jnp.bfloat16), tanh_part, sigmoid_part)


def own_rows(values):
    row_count = values.shape[0] // lax.axis_size("wt")
    return lax.dynamic_slice_in_dim(values, lax.axis_index("wt") * row_count, row_count, 0)


def mixing_short(signal, gated, mix_weight):
    partial_sum = jnp.dot(gated, mix_weight, preferred_element_type=jnp.float32)
    summed = lax.psum(partial_sum, "wt")
    return (signal.astype(jnp.float32) + summed).astype(jnp.bfloat16)


def mixing_long(signal, gated, mix_weight):
    shared = lax.psum_scatter(
        jnp.dot(gated, mix_weight, preferred_element_type=jnp.float32).astype(jnp.bfloat16),
        "wt",
        scatter_dimension=0,
        tiled=True,
    ).astype(jnp.float32)
    return (own_rows(signal).astype(jnp.float32) + shared).astype(jnp.bfloat16)


def gate_grads(upstream, mix_weight, gated, tanh_part, sigmoid_part):
    gated_grad = contract_cols(upstream, mix_weight)
    mix_grad = contract_rows(gated, upstream)
    filter_grad = gated_grad * sigmoid_part * (1.0 - tanh_part * tanh_part)
    gate_grad = gated_grad * tanh_part * sigmoid_part * (1.0 - sigmoid_part)
    return (jnp.concatenate([filter_grad, gate_grad], axis=1).astype(jnp.bfloat16), mix_grad)


def later_short(preact_grad):
    midpoint = preact_grad.shape[0] // 2
    packed = jnp.concatenate([preact_grad[:midpoint], preact_grad], axis=0)
    moved_rows = shifted(packed, "tm", -1)
    later_one = jnp.concatenate([preact_grad[midpoint:], moved_rows[:midpoint]], axis=0)
    return (later_one, moved_rows[midpoint:])


def later_long(preact_grad):
    later_one = shifted(preact_grad, "tm", -1)
    later_two = shifted(preact_grad, "tm", -2)
    return (later_one, later_two)


def finish_layer(
    stacked, preact_grad, later_one, later_two, tap_inputs, mix_grad, upstream, grad_scale
):
    back_sum = contract_cols(preact_grad, stacked[0])
    back_sum = back_sum + contract_cols(later_one, stacked[1])
    back_sum = back_sum + contract_cols(later_two, stacked[2])
    conv_grad = jnp.stack(
        [
            contract_rows(tap_inputs[0], preact_grad),
            contract_rows(tap_inputs[1], preact_grad),
            contract_rows(tap_inputs[2], preact_grad),
        ]
    )
    conv_total, mix_total = (
        lax.psum_scatter(conv_grad, "tm", scatter_dimension=1, tiled=True),
        lax.psum_scatter(mix_grad, "tm", scatter_dimension=1, tiled=True),
    )
    summed = lax.psum(back_sum, "wt")
    lowered = (upstream.astype(jnp.float32) + summed).astype(jnp.bfloat16)
    return (lowered, conv_total * grad_scale, mix_total * grad_scale)


def body(
    signal,
    cotangent,
    first_filter_taps,
    first_gate_taps,
    first_residual_projection,
    second_filter_taps,
    second_gate_taps,
    second_residual_projection,
):
    half_cols = first_filter_taps.shape[2]
    grad_scale = 1.0 / math.sqrt(signal.shape[0] * lax.axis_size("tm"))
    stacked_a = jnp.concatenate([first_filter_taps, first_gate_taps], axis=2)
    stacked_b = jnp.concatenate([second_filter_taps, second_gate_taps], axis=2)
    preact_a, taps_a = preact_short(signal, stacked_a)
    gated_output_first, tanh_branch_first, sigmoid_branch_first = gate_units(preact_a, half_cols)
    hidden_features = mixing_short(signal, gated_output_first, first_residual_projection)
    preact_b, taps_b = preact_long(hidden_features, stacked_b)
    gated_output_second, tanh_branch_second, sigmoid_branch_second = gate_units(preact_b, half_cols)
    second_layer_output = mixing_long(
        hidden_features, gated_output_second, second_residual_projection
    )
    pgrad_b, mixgrad_b = gate_grads(
        cotangent,
        second_residual_projection,
        gated_output_second,
        tanh_branch_second,
        sigmoid_branch_second,
    )
    later_one_b, later_two_b = later_long(pgrad_b)
    hidden_features_gradient, convolution_second_layer, projection_gradient_second = finish_layer(
        stacked_b, pgrad_b, later_one_b, later_two_b, taps_b, mixgrad_b, cotangent, grad_scale
    )
    pgrad_a, mixgrad_a = gate_grads(
        hidden_features_gradient,
        first_residual_projection,
        gated_output_first,
        tanh_branch_first,
        sigmoid_branch_first,
    )
    later_one_a, later_two_a = later_short(pgrad_a)
    input_feature_gradient, convolution_first_layer, projection_gradient_first = finish_layer(
        stacked_a,
        pgrad_a,
        later_one_a,
        later_two_a,
        taps_a,
        mixgrad_a,
        hidden_features_gradient,
        grad_scale,
    )
    return (
        second_layer_output,
        input_feature_gradient,
        convolution_first_layer[:, :, :half_cols],
        convolution_first_layer[:, :, half_cols:],
        projection_gradient_first,
        convolution_second_layer[:, :, :half_cols],
        convolution_second_layer[:, :, half_cols:],
        projection_gradient_second,
    )


def fused_kernel(
    tm, scale,
    sig, cot, f1, g1, m1, f2, g2, m2,
    o_out2, o_gx, o_cf1, o_cg1, o_mg1, o_cf2, o_cg2, o_mg2,
    sj, hj, w1, w2, a1, b1, gt1, a2, b2, gt2, gg, pre, pg1, pg2, hg, gxs,
    a_snd, a_rcv, b_snd, b_rcv, own, r_snd, r_rcv,
    w_snd, w_rcv, w_own, m_snd, m_rcv, m_own,
    load_sem, as_sem, ar_sem, bs_sem, br_sem, gs_sem, gr_sem,
    zs_sem, zr_sem, ws_sem, wr_sem, ms_sem, mr_sem,
):
    seg, chans = sig.shape
    quarter = seg // 4
    half_seg = seg // 2
    cols = f1.shape[2]
    cblk = chans // tm
    bf16, f32 = jnp.bfloat16, jnp.float32
    w = lax.axis_index("wt")
    z = lax.axis_index("tm")
    x, c = w // 2, w % 2
    mate = 2 * x + (1 - c)
    across = 2 * (1 - x) + c
    diag = 2 * (1 - x) + (1 - c)

    def rows(q, base=0):
        return pl.ds(pl.multiple_of(base + q * quarter, quarter), quarter)

    def dot(l, r):
        return jnp.dot(l, r, preferred_element_type=f32)

    def dot_t(l, r):
        return lax.dot_general(l, r, (((1,), (1,)), ((), ())), preferred_element_type=f32)

    def dot_rows(l, r):
        return lax.dot_general(l, r, (((0,), (0,)), ((), ())), preferred_element_type=f32)

    pending = []

    def remote(src, dst, ssem, rsem, target):
        return pltpu.make_async_remote_copy(
            src_ref=src, dst_ref=dst, send_sem=ssem, recv_sem=rsem,
            device_id=target, device_id_type=pl.DeviceIdType.MESH,
        )

    def go(copy, cond=None):
        pending.append((copy, cond))
        if cond is None:
            copy.start()
        else:
            pl.when(cond)(copy.start)

    def when(cond, fn):
        if cond is None:
            fn()
        else:
            pl.when(cond)(fn)

    loads = []
    for n, (layer, fil, gat) in enumerate(((w1, f1, g1), (w2, f2, g2))):
        for m, part in enumerate((fil, gat)):
            loads.append(
                pltpu.make_async_copy(
                    part, layer.at[:, :, m * cols : (m + 1) * cols], load_sem.at[2 * n + m]
                )
            )
    for load in loads:
        load.start()

    barrier = pltpu.get_barrier_semaphore()
    for peer in (mate, across):
        pl.semaphore_signal(
            barrier, inc=1, device_id={"wt": peer}, device_id_type=pl.DeviceIdType.MESH
        )
    for d in range(1, tm):
        pl.semaphore_signal(
            barrier, inc=1, device_id={"tm": lax.rem(z + d, tm)},
            device_id_type=pl.DeviceIdType.MESH,
        )
    pl.semaphore_wait(barrier, 2 + tm - 1)

    class Gather:
        def __init__(self, n, buf, base, cond=None):
            self.cond = cond
            mine, theirs = buf.at[rows(w, base)], buf.at[rows(across, base)]
            self.cross = remote(mine, mine, gs_sem.at[n, 0], gr_sem.at[n, 0], {"wt": across})
            self.near = remote(mine, mine, gs_sem.at[n, 1], gr_sem.at[n, 1], {"wt": mate})
            self.fwd = remote(theirs, theirs, gs_sem.at[n, 2], gr_sem.at[n, 2], {"wt": mate})

        def start(self):
            go(self.cross, self.cond)
            go(self.near, self.cond)

        def forward(self):
            when(self.cond, self.cross.wait_recv)
            go(self.fwd, self.cond)

        def finish(self):
            when(self.cond, self.near.wait_recv)
            when(self.cond, self.fwd.wait_recv)

    def a_copy(n, j):
        return remote(
            a_snd.at[n, j], a_rcv.at[n, j], as_sem.at[n, j], ar_sem.at[n, j], {"wt": mate}
        )

    def b_copy(n):
        return remote(b_snd.at[n], b_rcv.at[n], bs_sem.at[n], br_sem.at[n], {"wt": across})

    def rs_start(n, fn):
        for j, q in enumerate((diag, mate)):
            a_snd[n, j] = fn(q).astype(bf16)
            go(a_copy(n, j))
        for j, q in enumerate((across, w)):
            own[n, j] = fn(q)

    def rs_mid(n):
        a_copy(n, 0).wait_recv()
        b_snd[n] = (own[n, 0] + a_rcv[n, 0].astype(f32)).astype(bf16)
        go(b_copy(n))

    def rs_end(n):
        a_copy(n, 1).wait_recv()
        b_copy(n).wait_recv()
        return own[n, 1] + a_rcv[n, 1].astype(f32) + b_rcv[n].astype(f32)

    def z_copy(n, src, dst, step):
        return remote(
            src, dst, zs_sem.at[n], zr_sem.at[n], {"tm": lax.rem(z + step + tm, tm)}
        )

    halo = z_copy(0, sig.at[rows(w)], sj.at[rows(w)], 1)
    go(halo, z < tm - 1)
    sj[seg : 2 * seg] = sig[...]

    @pl.when(z == 0)
    def _():
        sj[0:seg] = jnp.zeros((seg, chans), bf16)
        hj[seg : 2 * seg] = jnp.zeros((seg, chans), bf16)

    @pl.when(z < 2)
    def _():
        hj[0:seg] = jnp.zeros((seg, chans), bf16)

    @pl.loop(0, 4)
    def _(r):
        gg[rows(r), :] = dot_t(cot[rows(r), :], m2[...])

    pl.when(z > 0)(halo.wait_recv)
    sig_gather = Gather(0, sj, 0, z > 0)
    sig_gather.start()
    loads[0].wait()
    loads[1].wait()

    @pl.loop(0, 4)
    def _(r):
        pre[rows(r), :] = dot(sj[rows(r, seg), :], w1[0])

    sig_gather.forward()
    sig_gather.finish()

    def gate(p, a_ref, b_ref, g_ref, q):
        a = jnp.tanh(p[:, :cols])
        b = jax.nn.sigmoid(p[:, cols:])
        a_ref[rows(q), :] = a
        b_ref[rows(q), :] = b
        g = (a * b).astype(bf16)
        g_ref[rows(q), :] = g
        return a, b, g

    def first_quarter(q):
        p = pre[rows(q), :] + dot(sj[rows(q, half_seg), :], w1[1]) + dot(sj[rows(q), :], w1[2])
        g = gate(p, a1, b1, gt1, q)[2]
        return dot(g, m1[...])

    rs_start(0, first_quarter)
    rs_mid(0)
    hj[rows(w, 2 * seg), :] = (sig[rows(w), :].astype(f32) + rs_end(0)).astype(bf16)

    g_own = Gather(1, hj, 2 * seg)
    one = z_copy(1, hj.at[rows(w, 2 * seg)], hj.at[rows(w, seg)], 1)
    two = z_copy(2, hj.at[rows(w, 2 * seg)], hj.at[rows(w)], 2)
    g_own.start()
    go(one, z < tm - 1)
    go(two, z < tm - 2)
    g_own.forward()
    pl.when(z > 0)(one.wait_recv)
    g_one = Gather(2, hj, seg, z > 0)
    g_one.start()
    g_own.finish()
    loads[2].wait()
    loads[3].wait()

    @pl.loop(0, 4)
    def _(r):
        pre[rows(r), :] = dot(hj[rows(r, 2 * seg), :], w2[0])

    g_one.forward()
    pl.when(z > 1)(two.wait_recv)
    g_two = Gather(3, hj, 0, z > 1)
    g_two.start()
    g_one.finish()

    @pl.loop(0, 4)
    def _(r):
        pre[rows(r), :] += dot(hj[rows(r, seg), :], w2[1])

    g_two.forward()
    g_two.finish()

    def pre_grad(gval, a, b, pg, q):
        pg[rows(q), 0:cols] = (gval * b * (1.0 - a * a)).astype(bf16)
        pg[rows(q), cols : 2 * cols] = (gval * a * b * (1.0 - b)).astype(bf16)

    @pl.loop(0, 4)
    def _(r):
        p = pre[rows(r), :] + dot(hj[rows(r), :], w2[2])
        a, b, _ = gate(p, a2, b2, gt2, r)
        pre_grad(gg[rows(r), :], a, b, pg2, r)

    rs_start(1, lambda q: dot_t(pg2[rows(q), :], w2[2]))
    rs_start(2, lambda q: dot_t(pg2[rows(q), :], w2[1]))
    rs_mid(1)
    rs_start(3, lambda q: dot_t(pg2[rows(q), :], w2[0]))
    rs_mid(2)
    rs_mid(3)

    def weight_blocks(n, taps, base, spread, pg, gated, up, d):
        j = lax.rem(z + d, tm)
        at = pl.ds(pl.multiple_of(j * cblk, cblk), cblk)
        for k in range(3):
            lo = base - spread * k
            block = dot_rows(taps[lo : lo + seg, at], pg[...])
            if d == 0:
                w_own[n, k * cblk : (k + 1) * cblk, :] = block
            else:
                w_snd[n, d - 1, k * cblk : (k + 1) * cblk, :] = block.astype(bf16)
        mix = dot_rows(gated[...], up[:, at])
        if d == 0:
            m_own[n] = mix
        else:
            m_snd[n, d - 1] = mix.astype(bf16)

    def w_copies(n, d):
        target = {"tm": lax.rem(z + d, tm)}
        s = d - 1
        return (
            remote(w_snd.at[n, s], w_rcv.at[n, s], ws_sem.at[n, s], wr_sem.at[n, s], target),
            remote(m_snd.at[n, s], m_rcv.at[n, s], ms_sem.at[n, s], mr_sem.at[n, s], target),
        )

    def weight_send(n, d):
        for copy in w_copies(n, d):
            go(copy)

    def weight_finish(n, o_f, o_g, o_m):
        for d in range(1, tm):
            for copy in w_copies(n, d):
                copy.wait_recv()
        for k in range(3):
            at = slice(k * cblk, (k + 1) * cblk)
            total = w_own[n, at, :]
            for d in range(1, tm):
                total = total + w_rcv[n, d - 1, at, :].astype(f32)
            total = total * scale
            o_f[k] = total[:, :cols]
            o_g[k] = total[:, cols:]
        total = m_own[n]
        for d in range(1, tm):
            total = total + m_rcv[n, d - 1].astype(f32)
        o_m[...] = total * scale

    second = (1, hj, 2 * seg, seg, pg2, gt2, cot)
    weight_blocks(*second, 1)
    r_snd[0] = rs_end(1).astype(bf16)
    back_two = z_copy(3, r_snd.at[0], r_rcv.at[0], -2)
    go(back_two, z > 1)
    r_snd[1] = rs_end(2).astype(bf16)
    back_one = z_copy(4, r_snd.at[1], r_rcv.at[1], -1)
    go(back_one, z > 0)
    weight_send(1, 1)
    for d in range(2, tm):
        weight_blocks(*second, d)
        weight_send(1, d)
    total = cot[rows(w), :].astype(f32) + rs_end(3)
    own[3, 0] = total

    @pl.when(z < tm - 1)
    def _():
        back_one.wait_recv()
        own[3, 0] += r_rcv[1].astype(f32)

    @pl.when(z < tm - 2)
    def _():
        back_two.wait_recv()
        own[3, 0] += r_rcv[0].astype(f32)

    hg[rows(w), :] = own[3, 0].astype(bf16)
    g_hg = Gather(4, hg, 0)
    g_hg.start()
    rs_start(4, lambda q: dot(gt2[rows(q), :], m2[...]))
    g_hg.forward()
    g_hg.finish()

    @pl.loop(0, 4)
    def _(r):
        gval = dot_t(hg[rows(r), :], m1[...])
        pre_grad(gval, a1[rows(r), :], b1[rows(r), :], pg1, r)

    def to_earlier(q):
        late = (q >= 2).astype(f32)
        shifted_q = lax.rem(q + 2, 4)
        return dot_t(pg1[rows(q), :], w1[2]) + late * dot_t(pg1[rows(shifted_q), :], w1[1])

    def to_here(q):
        early = (q < 2).astype(f32)
        shifted_q = lax.rem(q + 2, 4)
        return dot_t(pg1[rows(q), :], w1[0]) + early * dot_t(pg1[rows(shifted_q), :], w1[1])

    rs_start(5, to_earlier)
    rs_mid(5)
    rs_start(6, to_here)
    rs_mid(6)
    rs_mid(4)
    first = (0, sj, seg, half_seg, pg1, gt1, hg)
    weight_blocks(*first, 1)
    r_snd[2] = rs_end(5).astype(bf16)
    back_first = z_copy(5, r_snd.at[2], r_rcv.at[2], -1)
    go(back_first, z > 0)
    weight_send(0, 1)
    for d in range(2, tm):
        weight_blocks(*first, d)
        weight_send(0, d)
    own[6, 0] = hg[rows(w), :].astype(f32) + rs_end(6)

    @pl.when(z < tm - 1)
    def _():
        back_first.wait_recv()
        own[6, 0] += r_rcv[2].astype(f32)

    gxs[rows(w), :] = own[6, 0].astype(bf16)
    g_gx = Gather(5, gxs, 0)
    g_gx.start()
    weight_blocks(*second, 0)
    g_gx.forward()
    weight_blocks(*first, 0)
    o_out2[...] = (hj[rows(w, 2 * seg), :].astype(f32) + rs_end(4)).astype(bf16)
    g_gx.finish()
    o_gx[...] = gxs[...]
    weight_finish(1, o_cf2, o_cg2, o_mg2)
    weight_finish(0, o_cf1, o_cg1, o_mg1)
    for copy, cond in pending:
        when(cond, copy.wait_send)


def fused_body(*args):
    sig, cot, f1 = args[:3]
    seg, chans = sig.shape
    cols = f1.shape[2]
    tm = lax.axis_size("tm")
    quarter, cblk = seg // 4, chans // tm
    bf16, f32 = jnp.bfloat16, jnp.float32
    scale = 1.0 / math.sqrt(seg * tm)
    vm = pltpu.VMEM
    dma = pltpu.SemaphoreType.DMA
    wide, others = 2 * cols, tm - 1
    scratch = [
        vm((2 * seg, chans), bf16),
        vm((3 * seg, chans), bf16),
        vm((3, chans, wide), bf16),
        vm((3, chans, wide), bf16),
        vm((seg, cols), f32),
        vm((seg, cols), f32),
        vm((seg, cols), bf16),
        vm((seg, cols), f32),
        vm((seg, cols), f32),
        vm((seg, cols), bf16),
        vm((seg, cols), f32),
        vm((seg, wide), f32),
        vm((seg, wide), bf16),
        vm((seg, wide), bf16),
        vm((seg, chans), bf16),
        vm((seg, chans), bf16),
        vm((7, 2, quarter, chans), bf16),
        vm((7, 2, quarter, chans), bf16),
        vm((7, quarter, chans), bf16),
        vm((7, quarter, chans), bf16),
        vm((7, 2, quarter, chans), f32),
        vm((3, quarter, chans), bf16),
        vm((3, quarter, chans), bf16),
        vm((2, others, 3 * cblk, wide), bf16),
        vm((2, others, 3 * cblk, wide), bf16),
        vm((2, 3 * cblk, wide), f32),
        vm((2, others, cols, cblk), bf16),
        vm((2, others, cols, cblk), bf16),
        vm((2, cols, cblk), f32),
        dma((4,)),
        dma((7, 2)), dma((7, 2)), dma((7,)), dma((7,)),
        dma((6, 3)), dma((6, 3)),
        dma((6,)), dma((6,)),
        dma((2, others)), dma((2, others)), dma((2, others)), dma((2, others)),
    ]
    conv = jax.ShapeDtypeStruct((3, cblk, cols), f32)
    mix = jax.ShapeDtypeStruct((cols, cblk), f32)
    in_vm = pl.BlockSpec(memory_space=pltpu.VMEM)
    in_any = pl.BlockSpec(memory_space=pl.ANY)
    return pl.pallas_call(
        functools.partial(fused_kernel, tm, scale),
        out_shape=(
            jax.ShapeDtypeStruct((quarter, chans), bf16),
            jax.ShapeDtypeStruct((seg, chans), bf16),
            conv, conv, mix, conv, conv, mix,
        ),
        in_specs=[in_vm, in_vm, in_any, in_any, in_vm, in_any, in_any, in_vm],
        out_specs=(in_vm,) * 8,
        scratch_shapes=scratch,
        compiler_params=pltpu.CompilerParams(
            collective_id=0, has_side_effects=True, vmem_limit_bytes=56 * 1024 * 1024
        ),
    )(*args)


def fits(mesh):
    return mesh.shape["wt"] == 4 and 3 <= mesh.shape["tm"] <= 4


def solution(mesh):
    in_specs = (
        P(("grp", "tm"), None),
        P(("grp", "tm"), None),
        P(None, None, "wt"),
        P(None, None, "wt"),
        P("wt", None),
        P(None, None, "wt"),
        P(None, None, "wt"),
        P("wt", None),
    )
    out_specs = (
        P(("grp", "tm", "wt"), None),
        P(("grp", "tm"), None),
        P("grp", "tm", "wt"),
        P("grp", "tm", "wt"),
        P(("grp", "wt"), "tm"),
        P("grp", "tm", "wt"),
        P("grp", "tm", "wt"),
        P(("grp", "wt"), "tm"),
    )
    return jax.shard_map(fused_body if fits(mesh) else body, mesh=mesh, in_specs=in_specs, out_specs=out_specs, check_vma=False)
```

```python
import functools
import math

import jax
import jax.numpy as jnp
from jax import lax
from jax.experimental import pallas as pl
from jax.experimental.pallas import tpu as pltpu
from jax.sharding import PartitionSpec as P


def shifted(block, axis, distance):
    devices = range(lax.axis_size(axis))
    route = [(i - distance, i) for i in devices if i - distance in devices]
    return lax.ppermute(block, axis, route)


def contract_rows(left_side, right_side):
    return lax.dot_general(
        left_side, right_side, (((0,), (0,)), ((), ())), preferred_element_type=jnp.float32
    )


def contract_cols(left_side, right_side):
    return lax.dot_general(
        left_side, right_side, (((1,), (1,)), ((), ())), preferred_element_type=jnp.float32
    )


def apply_taps(tap_inputs, stacked):
    preact = jnp.dot(tap_inputs[0], stacked[0], preferred_element_type=jnp.float32)
    preact = preact + jnp.dot(tap_inputs[1], stacked[1], preferred_element_type=jnp.float32)
    return preact + jnp.dot(tap_inputs[2], stacked[2], preferred_element_type=jnp.float32)


def preact_short(signal, stacked):
    seg_rows = signal.shape[0]
    midpoint = seg_rows // 2
    earlier = shifted(signal, "tm", 1)
    joined = jnp.concatenate([earlier, signal], axis=0)
    tap_inputs = (signal, joined[midpoint : midpoint + seg_rows], earlier)
    return (apply_taps(tap_inputs, stacked), tap_inputs)


def preact_long(signal, stacked):
    one_back = shifted(signal, "tm", 1)
    two_back = shifted(signal, "tm", 2)
    tap_inputs = (signal, one_back, two_back)
    return (apply_taps(tap_inputs, stacked), tap_inputs)


def gate_units(preact, half_cols):
    tanh_part = jnp.tanh(preact[:, :half_cols])
    sigmoid_part = jax.nn.sigmoid(preact[:, half_cols:])
    return ((tanh_part * sigmoid_part).astype(jnp.bfloat16), tanh_part, sigmoid_part)


def own_rows(values):
    row_count = values.shape[0] // lax.axis_size("wt")
    return lax.dynamic_slice_in_dim(values, lax.axis_index("wt") * row_count, row_count, 0)


def mixing_short(signal, gated, mix_weight):
    partial_sum = jnp.dot(gated, mix_weight, preferred_element_type=jnp.float32)
    summed = lax.psum(partial_sum, "wt")
    return (signal.astype(jnp.float32) + summed).astype(jnp.bfloat16)


def mixing_long(signal, gated, mix_weight):
    shared = lax.psum_scatter(
        jnp.dot(gated, mix_weight, preferred_element_type=jnp.float32).astype(jnp.bfloat16),
        "wt",
        scatter_dimension=0,
        tiled=True,
    ).astype(jnp.float32)
    return (own_rows(signal).astype(jnp.float32) + shared).astype(jnp.bfloat16)


def gate_grads(upstream, mix_weight, gated, tanh_part, sigmoid_part):
    gated_grad = contract_cols(upstream, mix_weight)
    mix_grad = contract_rows(gated, upstream)
    filter_grad = gated_grad * sigmoid_part * (1.0 - tanh_part * tanh_part)
    gate_grad = gated_grad * tanh_part * sigmoid_part * (1.0 - sigmoid_part)
    return (jnp.concatenate([filter_grad, gate_grad], axis=1).astype(jnp.bfloat16), mix_grad)


def later_short(preact_grad):
    midpoint = preact_grad.shape[0] // 2
    packed = jnp.concatenate([preact_grad[:midpoint], preact_grad], axis=0)
    moved_rows = shifted(packed, "tm", -1)
    later_one = jnp.concatenate([preact_grad[midpoint:], moved_rows[:midpoint]], axis=0)
    return (later_one, moved_rows[midpoint:])


def later_long(preact_grad):
    later_one = shifted(preact_grad, "tm", -1)
    later_two = shifted(preact_grad, "tm", -2)
    return (later_one, later_two)


def finish_layer(
    stacked, preact_grad, later_one, later_two, tap_inputs, mix_grad, upstream, grad_scale
):
    back_sum = contract_cols(preact_grad, stacked[0])
    back_sum = back_sum + contract_cols(later_one, stacked[1])
    back_sum = back_sum + contract_cols(later_two, stacked[2])
    conv_grad = jnp.stack(
        [
            contract_rows(tap_inputs[0], preact_grad),
            contract_rows(tap_inputs[1], preact_grad),
            contract_rows(tap_inputs[2], preact_grad),
        ]
    )
    conv_total, mix_total = (
        lax.psum_scatter(conv_grad, "tm", scatter_dimension=1, tiled=True),
        lax.psum_scatter(mix_grad, "tm", scatter_dimension=1, tiled=True),
    )
    summed = lax.psum(back_sum, "wt")
    lowered = (upstream.astype(jnp.float32) + summed).astype(jnp.bfloat16)
    return (lowered, conv_total * grad_scale, mix_total * grad_scale)


def body(
    signal,
    cotangent,
    first_filter_taps,
    first_gate_taps,
    first_residual_projection,
    second_filter_taps,
    second_gate_taps,
    second_residual_projection,
):
    half_cols = first_filter_taps.shape[2]
    grad_scale = 1.0 / math.sqrt(signal.shape[0] * lax.axis_size("tm"))
    stacked_a = jnp.concatenate([first_filter_taps, first_gate_taps], axis=2)
    stacked_b = jnp.concatenate([second_filter_taps, second_gate_taps], axis=2)
    preact_a, taps_a = preact_short(signal, stacked_a)
    gated_output_first, tanh_branch_first, sigmoid_branch_first = gate_units(preact_a, half_cols)
    hidden_features = mixing_short(signal, gated_output_first, first_residual_projection)
    preact_b, taps_b = preact_long(hidden_features, stacked_b)
    gated_output_second, tanh_branch_second, sigmoid_branch_second = gate_units(preact_b, half_cols)
    second_layer_output = mixing_long(
        hidden_features, gated_output_second, second_residual_projection
    )
    pgrad_b, mixgrad_b = gate_grads(
        cotangent,
        second_residual_projection,
        gated_output_second,
        tanh_branch_second,
        sigmoid_branch_second,
    )
    later_one_b, later_two_b = later_long(pgrad_b)
    hidden_features_gradient, convolution_second_layer, projection_gradient_second = finish_layer(
        stacked_b, pgrad_b, later_one_b, later_two_b, taps_b, mixgrad_b, cotangent, grad_scale
    )
    pgrad_a, mixgrad_a = gate_grads(
        hidden_features_gradient,
        first_residual_projection,
        gated_output_first,
        tanh_branch_first,
        sigmoid_branch_first,
    )
    later_one_a, later_two_a = later_short(pgrad_a)
    input_feature_gradient, convolution_first_layer, projection_gradient_first = finish_layer(
        stacked_a,
        pgrad_a,
        later_one_a,
        later_two_a,
        taps_a,
        mixgrad_a,
        hidden_features_gradient,
        grad_scale,
    )
    return (
        second_layer_output,
        input_feature_gradient,
        convolution_first_layer[:, :, :half_cols],
        convolution_first_layer[:, :, half_cols:],
        projection_gradient_first,
        convolution_second_layer[:, :, :half_cols],
        convolution_second_layer[:, :, half_cols:],
        projection_gradient_second,
    )


def fused_kernel(
    tm, scale,
    sig, cot, f1, g1, m1, f2, g2, m2,
    o_out2, o_gx, o_cf1, o_cg1, o_mg1, o_cf2, o_cg2, o_mg2,
    sj, hj, w1, w2, a1, b1, gt1, a2, b2, gt2, gg, pre, pg1, pg2, hg, gxs,
    a_snd, a_rcv, b_snd, b_rcv, own, r_snd, r_rcv,
    w_snd, w_rcv, w_own, w_far, m_snd, m_rcv, m_own, m_far,
    load_sem, as_sem, ar_sem, bs_sem, br_sem, gs_sem, gr_sem,
    zs_sem, zr_sem, ws_sem, wr_sem, ms_sem, mr_sem,
):
    seg, chans = sig.shape
    quarter = seg // 4
    half_seg = seg // 2
    cols = f1.shape[2]
    cblk = chans // tm
    bf16, f32 = jnp.bfloat16, jnp.float32
    w = lax.axis_index("wt")
    z = lax.axis_index("tm")
    x, c = w // 2, w % 2
    mate = 2 * x + (1 - c)
    across = 2 * (1 - x) + c
    diag = 2 * (1 - x) + (1 - c)

    def rows(q, base=0):
        return pl.ds(pl.multiple_of(base + q * quarter, quarter), quarter)

    def dot(l, r):
        return jnp.dot(l, r, preferred_element_type=f32)

    def dot_t(l, r):
        return lax.dot_general(l, r, (((1,), (1,)), ((), ())), preferred_element_type=f32)

    def dot_rows(l, r):
        return lax.dot_general(l, r, (((0,), (0,)), ((), ())), preferred_element_type=f32)

    pending = []

    def remote(src, dst, ssem, rsem, target):
        return pltpu.make_async_remote_copy(
            src_ref=src, dst_ref=dst, send_sem=ssem, recv_sem=rsem,
            device_id=target, device_id_type=pl.DeviceIdType.MESH,
        )

    def go(copy, cond=None):
        pending.append((copy, cond))
        if cond is None:
            copy.start()
        else:
            pl.when(cond)(copy.start)

    def when(cond, fn):
        if cond is None:
            fn()
        else:
            pl.when(cond)(fn)

    loads = []
    for n, (layer, fil, gat) in enumerate(((w1, f1, g1), (w2, f2, g2))):
        for m, part in enumerate((fil, gat)):
            loads.append(
                pltpu.make_async_copy(
                    part, layer.at[:, :, m * cols : (m + 1) * cols], load_sem.at[2 * n + m]
                )
            )
    for load in loads:
        load.start()

    barrier = pltpu.get_barrier_semaphore()
    for peer in (mate, across):
        pl.semaphore_signal(
            barrier, inc=1, device_id={"wt": peer}, device_id_type=pl.DeviceIdType.MESH
        )
    for d in range(1, tm):
        pl.semaphore_signal(
            barrier, inc=1, device_id={"tm": lax.rem(z + d, tm)},
            device_id_type=pl.DeviceIdType.MESH,
        )
    pl.semaphore_wait(barrier, 2 + tm - 1)

    class Gather:
        def __init__(self, n, buf, base, cond=None):
            self.cond = cond
            mine, theirs = buf.at[rows(w, base)], buf.at[rows(across, base)]
            self.cross = remote(mine, mine, gs_sem.at[n, 0], gr_sem.at[n, 0], {"wt": across})
            self.near = remote(mine, mine, gs_sem.at[n, 1], gr_sem.at[n, 1], {"wt": mate})
            self.fwd = remote(theirs, theirs, gs_sem.at[n, 2], gr_sem.at[n, 2], {"wt": mate})

        def start(self):
            go(self.cross, self.cond)
            go(self.near, self.cond)

        def forward(self):
            when(self.cond, self.cross.wait_recv)
            go(self.fwd, self.cond)

        def finish(self):
            when(self.cond, self.near.wait_recv)
            when(self.cond, self.fwd.wait_recv)

    def a_copy(n, j):
        return remote(
            a_snd.at[n, j], a_rcv.at[n, j], as_sem.at[n, j], ar_sem.at[n, j], {"wt": mate}
        )

    def b_copy(n):
        return remote(b_snd.at[n], b_rcv.at[n], bs_sem.at[n], br_sem.at[n], {"wt": across})

    def rs_start(n, fn):
        for j, q in enumerate((diag, mate)):
            a_snd[n, j] = fn(q).astype(bf16)
            go(a_copy(n, j))
        for j, q in enumerate((across, w)):
            own[n, j] = fn(q)

    def rs_mid(n):
        a_copy(n, 0).wait_recv()
        b_snd[n] = (own[n, 0] + a_rcv[n, 0].astype(f32)).astype(bf16)
        go(b_copy(n))

    def rs_end(n):
        a_copy(n, 1).wait_recv()
        b_copy(n).wait_recv()
        return own[n, 1] + a_rcv[n, 1].astype(f32) + b_rcv[n].astype(f32)

    def z_copy(n, src, dst, step):
        return remote(
            src, dst, zs_sem.at[n], zr_sem.at[n], {"tm": lax.rem(z + step + tm, tm)}
        )

    def inner_of(i):
        return jnp.logical_and(i > 0, i < tm - 1)

    halo = z_copy(0, sig.at[rows(w)], sj.at[rows(w)], 1)
    go(halo, z < tm - 1)
    sj[seg : 2 * seg] = sig[...]

    @pl.when(z == 0)
    def _():
        sj[0:seg] = jnp.zeros((seg, chans), bf16)
        hj[seg : 2 * seg] = jnp.zeros((seg, chans), bf16)

    @pl.when(z < 2)
    def _():
        hj[0:seg] = jnp.zeros((seg, chans), bf16)

    @pl.loop(0, 4)
    def _(r):
        gg[rows(r), :] = dot_t(cot[rows(r), :], m2[...])

    pl.when(z > 0)(halo.wait_recv)
    sig_gather = Gather(0, sj, 0, z > 0)
    sig_gather.start()
    loads[0].wait()
    loads[1].wait()

    @pl.loop(0, 4)
    def _(r):
        pre[rows(r), :] = dot(sj[rows(r, seg), :], w1[0])

    sig_gather.forward()
    sig_gather.finish()

    def gate(p, a_ref, b_ref, g_ref, q):
        a = jnp.tanh(p[:, :cols])
        b = jax.nn.sigmoid(p[:, cols:])
        a_ref[rows(q), :] = a
        b_ref[rows(q), :] = b
        g = (a * b).astype(bf16)
        g_ref[rows(q), :] = g
        return a, b, g

    def first_quarter(q):
        p = pre[rows(q), :] + dot(sj[rows(q, half_seg), :], w1[1]) + dot(sj[rows(q), :], w1[2])
        g = gate(p, a1, b1, gt1, q)[2]
        return dot(g, m1[...])

    rs_start(0, first_quarter)
    rs_mid(0)
    hj[rows(w, 2 * seg), :] = (sig[rows(w), :].astype(f32) + rs_end(0)).astype(bf16)

    g_own = Gather(1, hj, 2 * seg)
    one = z_copy(1, hj.at[rows(w, 2 * seg)], hj.at[rows(w, seg)], 1)
    two = z_copy(2, hj.at[rows(w, seg)], hj.at[rows(w)], 1)
    g_own.start()
    go(one, z < tm - 1)
    g_own.forward()
    pl.when(z > 0)(one.wait_recv)
    go(two, inner_of(z))
    g_one = Gather(2, hj, seg, z > 0)
    g_one.start()
    g_own.finish()
    loads[2].wait()
    loads[3].wait()

    @pl.loop(0, 4)
    def _(r):
        pre[rows(r), :] = dot(hj[rows(r, 2 * seg), :], w2[0])

    g_one.forward()
    pl.when(z > 1)(two.wait_recv)
    g_two = Gather(3, hj, 0, z > 1)
    g_two.start()
    g_one.finish()

    @pl.loop(0, 4)
    def _(r):
        pre[rows(r), :] += dot(hj[rows(r, seg), :], w2[1])

    g_two.forward()
    g_two.finish()

    def pre_grad(gval, a, b, pg, q):
        pg[rows(q), 0:cols] = (gval * b * (1.0 - a * a)).astype(bf16)
        pg[rows(q), cols : 2 * cols] = (gval * a * b * (1.0 - b)).astype(bf16)

    @pl.loop(0, 4)
    def _(r):
        p = pre[rows(r), :] + dot(hj[rows(r), :], w2[2])
        a, b, _ = gate(p, a2, b2, gt2, r)
        pre_grad(gg[rows(r), :], a, b, pg2, r)

    rs_start(1, lambda q: dot_t(pg2[rows(q), :], w2[2]))
    rs_start(2, lambda q: dot_t(pg2[rows(q), :], w2[1]))
    rs_mid(1)
    rs_start(3, lambda q: dot_t(pg2[rows(q), :], w2[0]))
    rs_mid(2)
    rs_mid(3)

    low = z < 2
    inner = inner_of(z)
    outer = jnp.logical_not(inner)
    far_end = jnp.where(low, tm - 1, 0)
    block_of = (
        far_end,
        jnp.where(low, 2, 1),
        jnp.where(z == 0, 1, jnp.where(z == 1, 0, jnp.where(z == 2, 3, 2))),
        z,
    )
    target_of = (
        jnp.where(z == 0, 1, jnp.where(z == tm - 1, 2, far_end)), block_of[1], block_of[2]
    )
    middle_slot = jnp.where(inner, 2, 3)
    land_of = (0, middle_slot, 1)

    def weight_blocks(n, taps, base, spread, pg, gated, up, slot):
        j = block_of[slot]
        at = pl.ds(pl.multiple_of(j * cblk, cblk), cblk)
        mix = dot_rows(gated[...], up[:, at])
        if slot == 0:
            m_far[n] = mix
        if slot == 3:
            m_own[n] = mix
        else:
            m_snd[n, slot] = mix.astype(bf16)
        for k in range(3):
            lo = base - spread * k
            block = dot_rows(taps[lo : lo + seg, at], pg[...])
            if slot == 0:
                w_far[n, k * cblk : (k + 1) * cblk, :] = block
            if slot == 3:
                w_own[n, k * cblk : (k + 1) * cblk, :] = block
            else:
                w_snd[n, slot, k * cblk : (k + 1) * cblk, :] = block.astype(bf16)

    def w_copies(n, slot, land):
        target = {"tm": target_of[slot]}
        return (
            remote(
                w_snd.at[n, slot], w_rcv.at[n, land], ws_sem.at[n, slot], wr_sem.at[n, land], target
            ),
            remote(
                m_snd.at[n, slot], m_rcv.at[n, land], ms_sem.at[n, slot], mr_sem.at[n, land], target
            ),
        )

    def weight_send(n, slot):
        for copy in w_copies(n, slot, land_of[slot]):
            if slot > 0:
                go(copy)
            else:
                go(copy, outer)

    def weight_relay(n):
        copies = w_copies(n, 0, 0)

        @pl.when(inner)
        def _():
            for copy in copies:
                copy.wait_recv()
            w_snd[n, 0] = (w_far[n] + w_rcv[n, 0].astype(f32)).astype(bf16)
            m_snd[n, 0] = (m_far[n] + m_rcv[n, 0].astype(f32)).astype(bf16)

        for copy in copies:
            go(copy, inner)

    def weight_finish(n, o_f, o_g, o_m):
        def take(land):
            for copy in w_copies(n, 0, land):
                copy.wait_recv()
            w_own[n] += w_rcv[n, land].astype(f32)
            m_own[n] += m_rcv[n, land].astype(f32)

        take(1)

        @pl.when(inner)
        def _():
            take(2)
            take(3)

        @pl.when(outer)
        def _():
            take(0)

        for k in range(3):
            total = w_own[n, k * cblk : (k + 1) * cblk, :] * scale
            o_f[k] = total[:, :cols]
            o_g[k] = total[:, cols:]
        o_m[...] = m_own[n] * scale

    second = (1, hj, 2 * seg, seg, pg2, gt2, cot)
    weight_blocks(*second, 0)
    r_snd[0] = rs_end(1).astype(bf16)
    back_two = z_copy(3, r_snd.at[0], r_rcv.at[0], -1)
    go(back_two, z > 1)
    weight_blocks(*second, 1)
    own[2, 0] = rs_end(2)

    @pl.when(inner_of(z))
    def _():
        back_two.wait_recv()
        own[2, 0] += r_rcv[0].astype(f32)

    r_snd[1] = own[2, 0].astype(bf16)
    back_one = z_copy(4, r_snd.at[1], r_rcv.at[1], -1)
    go(back_one, z > 0)
    weight_send(1, 0)
    weight_send(1, 1)
    weight_blocks(*second, 2)
    weight_send(1, 2)
    own[3, 0] = cot[rows(w), :].astype(f32) + rs_end(3)

    @pl.when(z < tm - 1)
    def _():
        back_one.wait_recv()
        own[3, 0] += r_rcv[1].astype(f32)

    hg[rows(w), :] = own[3, 0].astype(bf16)
    g_hg = Gather(4, hg, 0)
    g_hg.start()
    rs_start(4, lambda q: dot(gt2[rows(q), :], m2[...]))
    g_hg.forward()
    g_hg.finish()

    @pl.loop(0, 4)
    def _(r):
        gval = dot_t(hg[rows(r), :], m1[...])
        pre_grad(gval, a1[rows(r), :], b1[rows(r), :], pg1, r)

    def to_earlier(q):
        late = (q >= 2).astype(f32)
        shifted_q = lax.rem(q + 2, 4)
        return dot_t(pg1[rows(q), :], w1[2]) + late * dot_t(pg1[rows(shifted_q), :], w1[1])

    def to_here(q):
        early = (q < 2).astype(f32)
        shifted_q = lax.rem(q + 2, 4)
        return dot_t(pg1[rows(q), :], w1[0]) + early * dot_t(pg1[rows(shifted_q), :], w1[1])

    rs_start(5, to_earlier)
    rs_mid(5)
    rs_start(6, to_here)
    rs_mid(6)
    rs_mid(4)
    first = (0, sj, seg, half_seg, pg1, gt1, hg)
    weight_blocks(*first, 0)
    r_snd[2] = rs_end(5).astype(bf16)
    back_first = z_copy(5, r_snd.at[2], r_rcv.at[2], -1)
    go(back_first, z > 0)
    weight_send(0, 0)
    weight_blocks(*first, 1)
    weight_send(0, 1)
    weight_relay(1)
    weight_blocks(*first, 2)
    weight_send(0, 2)
    own[6, 0] = hg[rows(w), :].astype(f32) + rs_end(6)

    @pl.when(z < tm - 1)
    def _():
        back_first.wait_recv()
        own[6, 0] += r_rcv[2].astype(f32)

    gxs[rows(w), :] = own[6, 0].astype(bf16)
    g_gx = Gather(5, gxs, 0)
    g_gx.start()
    weight_blocks(*second, 3)
    g_gx.forward()
    weight_blocks(*first, 3)
    o_out2[...] = (hj[rows(w, 2 * seg), :].astype(f32) + rs_end(4)).astype(bf16)
    g_gx.finish()
    o_gx[...] = gxs[...]
    weight_relay(0)
    weight_finish(1, o_cf2, o_cg2, o_mg2)
    weight_finish(0, o_cf1, o_cg1, o_mg1)
    for copy, cond in pending:
        when(cond, copy.wait_send)


def hand_over(*refs):
    for n in range(8):
        refs[8 + n][...] = refs[n][...]


def fused_body(*args):
    sig, cot, f1 = args[:3]
    seg, chans = sig.shape
    cols = f1.shape[2]
    tm = lax.axis_size("tm")
    quarter, cblk = seg // 4, chans // tm
    bf16, f32 = jnp.bfloat16, jnp.float32
    scale = 1.0 / math.sqrt(seg * tm)
    vm = pltpu.VMEM
    dma = pltpu.SemaphoreType.DMA
    wide = 2 * cols
    scratch = [
        vm((2 * seg, chans), bf16),
        vm((3 * seg, chans), bf16),
        vm((3, chans, wide), bf16),
        vm((3, chans, wide), bf16),
        vm((seg, cols), f32),
        vm((seg, cols), f32),
        vm((seg, cols), bf16),
        vm((seg, cols), f32),
        vm((seg, cols), f32),
        vm((seg, cols), bf16),
        vm((seg, cols), f32),
        vm((seg, wide), f32),
        vm((seg, wide), bf16),
        vm((seg, wide), bf16),
        vm((seg, chans), bf16),
        vm((seg, chans), bf16),
        vm((7, 2, quarter, chans), bf16),
        vm((7, 2, quarter, chans), bf16),
        vm((7, quarter, chans), bf16),
        vm((7, quarter, chans), bf16),
        vm((7, 2, quarter, chans), f32),
        vm((3, quarter, chans), bf16),
        vm((3, quarter, chans), bf16),
        vm((2, 3, 3 * cblk, wide), bf16),
        vm((2, 4, 3 * cblk, wide), bf16),
        vm((2, 3 * cblk, wide), f32),
        vm((2, 3 * cblk, wide), f32),
        vm((2, 3, cols, cblk), bf16),
        vm((2, 4, cols, cblk), bf16),
        vm((2, cols, cblk), f32),
        vm((2, cols, cblk), f32),
        dma((4,)),
        dma((7, 2)), dma((7, 2)), dma((7,)), dma((7,)),
        dma((6, 3)), dma((6, 3)),
        dma((6,)), dma((6,)),
        dma((2, 3)), dma((2, 4)), dma((2, 3)), dma((2, 4)),
    ]
    conv = jax.ShapeDtypeStruct((3, cblk, cols), f32)
    mix = jax.ShapeDtypeStruct((cols, cblk), f32)
    in_vm = pl.BlockSpec(memory_space=pltpu.VMEM)
    in_any = pl.BlockSpec(memory_space=pl.ANY)
    shapes = (
        jax.ShapeDtypeStruct((quarter, chans), bf16),
        jax.ShapeDtypeStruct((seg, chans), bf16),
        conv, conv, mix, conv, conv, mix,
    )
    results = pl.pallas_call(
        functools.partial(fused_kernel, tm, scale),
        out_shape=shapes,
        in_specs=[in_vm, in_vm, in_any, in_any, in_vm, in_any, in_any, in_vm],
        out_specs=(in_vm,) * 8,
        scratch_shapes=scratch,
        compiler_params=pltpu.CompilerParams(
            collective_id=0, has_side_effects=True, vmem_limit_bytes=56 * 1024 * 1024
        ),
    )(*args)
    return pl.pallas_call(
        hand_over,
        out_shape=shapes,
        in_specs=[in_vm] * 8,
        out_specs=(in_vm,) * 8,
    )(*results)


def fits(mesh):
    return mesh.shape["wt"] == 4 and mesh.shape["tm"] == 4


def solution(mesh):
    in_specs = (
        P(("grp", "tm"), None),
        P(("grp", "tm"), None),
        P(None, None, "wt"),
        P(None, None, "wt"),
        P("wt", None),
        P(None, None, "wt"),
        P(None, None, "wt"),
        P("wt", None),
    )
    out_specs = (
        P(("grp", "tm", "wt"), None),
        P(("grp", "tm"), None),
        P("grp", "tm", "wt"),
        P("grp", "tm", "wt"),
        P(("grp", "wt"), "tm"),
        P("grp", "tm", "wt"),
        P("grp", "tm", "wt"),
        P(("grp", "wt"), "tm"),
    )
    return jax.shard_map(fused_body if fits(mesh) else body, mesh=mesh, in_specs=in_specs, out_specs=out_specs, check_vma=False)
```

```python
import functools
import math

import jax
import jax.numpy as jnp
from jax import lax
from jax.experimental import pallas as pl
from jax.experimental.pallas import tpu as pltpu
from jax.sharding import PartitionSpec as P


def shifted(block, axis, distance):
    devices = range(lax.axis_size(axis))
    route = [(i - distance, i) for i in devices if i - distance in devices]
    return lax.ppermute(block, axis, route)


def contract_rows(left_side, right_side):
    return lax.dot_general(
        left_side, right_side, (((0,), (0,)), ((), ())), preferred_element_type=jnp.float32
    )


def contract_cols(left_side, right_side):
    return lax.dot_general(
        left_side, right_side, (((1,), (1,)), ((), ())), preferred_element_type=jnp.float32
    )


def apply_taps(tap_inputs, stacked):
    preact = jnp.dot(tap_inputs[0], stacked[0], preferred_element_type=jnp.float32)
    preact = preact + jnp.dot(tap_inputs[1], stacked[1], preferred_element_type=jnp.float32)
    return preact + jnp.dot(tap_inputs[2], stacked[2], preferred_element_type=jnp.float32)


def preact_short(signal, stacked):
    seg_rows = signal.shape[0]
    midpoint = seg_rows // 2
    earlier = shifted(signal, "tm", 1)
    joined = jnp.concatenate([earlier, signal], axis=0)
    tap_inputs = (signal, joined[midpoint : midpoint + seg_rows], earlier)
    return (apply_taps(tap_inputs, stacked), tap_inputs)


def preact_long(signal, stacked):
    one_back = shifted(signal, "tm", 1)
    two_back = shifted(signal, "tm", 2)
    tap_inputs = (signal, one_back, two_back)
    return (apply_taps(tap_inputs, stacked), tap_inputs)


def gate_units(preact, half_cols):
    tanh_part = jnp.tanh(preact[:, :half_cols])
    sigmoid_part = jax.nn.sigmoid(preact[:, half_cols:])
    return ((tanh_part * sigmoid_part).astype(jnp.bfloat16), tanh_part, sigmoid_part)


def own_rows(values):
    row_count = values.shape[0] // lax.axis_size("wt")
    return lax.dynamic_slice_in_dim(values, lax.axis_index("wt") * row_count, row_count, 0)


def mixing_short(signal, gated, mix_weight):
    partial_sum = jnp.dot(gated, mix_weight, preferred_element_type=jnp.float32)
    summed = lax.psum(partial_sum, "wt")
    return (signal.astype(jnp.float32) + summed).astype(jnp.bfloat16)


def mixing_long(signal, gated, mix_weight):
    shared = lax.psum_scatter(
        jnp.dot(gated, mix_weight, preferred_element_type=jnp.float32).astype(jnp.bfloat16),
        "wt",
        scatter_dimension=0,
        tiled=True,
    ).astype(jnp.float32)
    return (own_rows(signal).astype(jnp.float32) + shared).astype(jnp.bfloat16)


def gate_grads(upstream, mix_weight, gated, tanh_part, sigmoid_part):
    gated_grad = contract_cols(upstream, mix_weight)
    mix_grad = contract_rows(gated, upstream)
    filter_grad = gated_grad * sigmoid_part * (1.0 - tanh_part * tanh_part)
    gate_grad = gated_grad * tanh_part * sigmoid_part * (1.0 - sigmoid_part)
    return (jnp.concatenate([filter_grad, gate_grad], axis=1).astype(jnp.bfloat16), mix_grad)


def later_short(preact_grad):
    midpoint = preact_grad.shape[0] // 2
    packed = jnp.concatenate([preact_grad[:midpoint], preact_grad], axis=0)
    moved_rows = shifted(packed, "tm", -1)
    later_one = jnp.concatenate([preact_grad[midpoint:], moved_rows[:midpoint]], axis=0)
    return (later_one, moved_rows[midpoint:])


def later_long(preact_grad):
    later_one = shifted(preact_grad, "tm", -1)
    later_two = shifted(preact_grad, "tm", -2)
    return (later_one, later_two)


def finish_layer(
    stacked, preact_grad, later_one, later_two, tap_inputs, mix_grad, upstream, grad_scale
):
    back_sum = contract_cols(preact_grad, stacked[0])
    back_sum = back_sum + contract_cols(later_one, stacked[1])
    back_sum = back_sum + contract_cols(later_two, stacked[2])
    conv_grad = jnp.stack(
        [
            contract_rows(tap_inputs[0], preact_grad),
            contract_rows(tap_inputs[1], preact_grad),
            contract_rows(tap_inputs[2], preact_grad),
        ]
    )
    conv_total, mix_total = (
        lax.psum_scatter(conv_grad, "tm", scatter_dimension=1, tiled=True),
        lax.psum_scatter(mix_grad, "tm", scatter_dimension=1, tiled=True),
    )
    summed = lax.psum(back_sum, "wt")
    lowered = (upstream.astype(jnp.float32) + summed).astype(jnp.bfloat16)
    return (lowered, conv_total * grad_scale, mix_total * grad_scale)


def body(
    signal,
    cotangent,
    first_filter_taps,
    first_gate_taps,
    first_residual_projection,
    second_filter_taps,
    second_gate_taps,
    second_residual_projection,
):
    half_cols = first_filter_taps.shape[2]
    grad_scale = 1.0 / math.sqrt(signal.shape[0] * lax.axis_size("tm"))
    stacked_a = jnp.concatenate([first_filter_taps, first_gate_taps], axis=2)
    stacked_b = jnp.concatenate([second_filter_taps, second_gate_taps], axis=2)
    preact_a, taps_a = preact_short(signal, stacked_a)
    gated_output_first, tanh_branch_first, sigmoid_branch_first = gate_units(preact_a, half_cols)
    hidden_features = mixing_short(signal, gated_output_first, first_residual_projection)
    preact_b, taps_b = preact_long(hidden_features, stacked_b)
    gated_output_second, tanh_branch_second, sigmoid_branch_second = gate_units(preact_b, half_cols)
    second_layer_output = mixing_long(
        hidden_features, gated_output_second, second_residual_projection
    )
    pgrad_b, mixgrad_b = gate_grads(
        cotangent,
        second_residual_projection,
        gated_output_second,
        tanh_branch_second,
        sigmoid_branch_second,
    )
    later_one_b, later_two_b = later_long(pgrad_b)
    hidden_features_gradient, convolution_second_layer, projection_gradient_second = finish_layer(
        stacked_b, pgrad_b, later_one_b, later_two_b, taps_b, mixgrad_b, cotangent, grad_scale
    )
    pgrad_a, mixgrad_a = gate_grads(
        hidden_features_gradient,
        first_residual_projection,
        gated_output_first,
        tanh_branch_first,
        sigmoid_branch_first,
    )
    later_one_a, later_two_a = later_short(pgrad_a)
    input_feature_gradient, convolution_first_layer, projection_gradient_first = finish_layer(
        stacked_a,
        pgrad_a,
        later_one_a,
        later_two_a,
        taps_a,
        mixgrad_a,
        hidden_features_gradient,
        grad_scale,
    )
    return (
        second_layer_output,
        input_feature_gradient,
        convolution_first_layer[:, :, :half_cols],
        convolution_first_layer[:, :, half_cols:],
        projection_gradient_first,
        convolution_second_layer[:, :, :half_cols],
        convolution_second_layer[:, :, half_cols:],
        projection_gradient_second,
    )


def fused_kernel(
    tm, scale,
    sig, cot, f1, g1, m1, f2, g2, m2,
    o_out2, o_gx, o_cf1, o_cg1, o_mg1, o_cf2, o_cg2, o_mg2,
    sj, hj, w1, w2, a1, b1, gt1, a2, b2, gt2, gg, pre, pg1, pg2, hg, gxs,
    a_snd, a_rcv, b_snd, b_rcv, own, r_snd, r_rcv,
    w_snd, w_rcv, w_own, w_far, m_snd, m_rcv, m_own, m_far,
    load_sem, as_sem, ar_sem, bs_sem, br_sem, gs_sem, gr_sem,
    zs_sem, zr_sem, ws_sem, wr_sem, ms_sem, mr_sem,
):
    seg, chans = sig.shape
    quarter = seg // 4
    half_seg = seg // 2
    cols = f1.shape[2]
    cblk = chans // tm
    bf16, f32 = jnp.bfloat16, jnp.float32
    w = lax.axis_index("wt")
    z = lax.axis_index("tm")
    x, c = w // 2, w % 2
    mate = 2 * x + (1 - c)
    across = 2 * (1 - x) + c
    diag = 2 * (1 - x) + (1 - c)

    def rows(q, base=0):
        return pl.ds(pl.multiple_of(base + q * quarter, quarter), quarter)

    def dot(l, r):
        return jnp.dot(l, r, preferred_element_type=f32)

    def dot_t(l, r):
        return lax.dot_general(l, r, (((1,), (1,)), ((), ())), preferred_element_type=f32)

    def dot_rows(l, r):
        return lax.dot_general(l, r, (((0,), (0,)), ((), ())), preferred_element_type=f32)

    pending = []

    def remote(src, dst, ssem, rsem, target):
        return pltpu.make_async_remote_copy(
            src_ref=src, dst_ref=dst, send_sem=ssem, recv_sem=rsem,
            device_id=target, device_id_type=pl.DeviceIdType.MESH,
        )

    def go(copy, cond=None):
        pending.append((copy, cond))
        if cond is None:
            copy.start()
        else:
            pl.when(cond)(copy.start)

    def when(cond, fn):
        if cond is None:
            fn()
        else:
            pl.when(cond)(fn)

    loads = []
    for n, (layer, fil, gat) in enumerate(((w1, f1, g1), (w2, f2, g2))):
        for m, part in enumerate((fil, gat)):
            loads.append(
                pltpu.make_async_copy(
                    part, layer.at[:, :, m * cols : (m + 1) * cols], load_sem.at[2 * n + m]
                )
            )
    for load in loads:
        load.start()

    barrier = pltpu.get_barrier_semaphore()
    for peer in (mate, across):
        pl.semaphore_signal(
            barrier, inc=1, device_id={"wt": peer}, device_id_type=pl.DeviceIdType.MESH
        )
    for d in range(1, tm):
        pl.semaphore_signal(
            barrier, inc=1, device_id={"tm": lax.rem(z + d, tm)},
            device_id_type=pl.DeviceIdType.MESH,
        )
    pl.semaphore_wait(barrier, 2 + tm - 1)

    class Gather:
        def __init__(self, n, buf, base, cond=None):
            self.cond = cond
            mine, theirs = buf.at[rows(w, base)], buf.at[rows(across, base)]
            self.cross = remote(mine, mine, gs_sem.at[n, 0], gr_sem.at[n, 0], {"wt": across})
            self.near = remote(mine, mine, gs_sem.at[n, 1], gr_sem.at[n, 1], {"wt": mate})
            self.fwd = remote(theirs, theirs, gs_sem.at[n, 2], gr_sem.at[n, 2], {"wt": mate})

        def start(self):
            go(self.cross, self.cond)
            go(self.near, self.cond)

        def forward(self):
            when(self.cond, self.cross.wait_recv)
            go(self.fwd, self.cond)

        def finish(self):
            when(self.cond, self.near.wait_recv)
            when(self.cond, self.fwd.wait_recv)

    def a_copy(n, j):
        return remote(
            a_snd.at[n, j], a_rcv.at[n, j], as_sem.at[n, j], ar_sem.at[n, j], {"wt": mate}
        )

    def b_copy(n):
        return remote(b_snd.at[n], b_rcv.at[n], bs_sem.at[n], br_sem.at[n], {"wt": across})

    def rs_start(n, fn):
        for j, q in enumerate((diag, mate)):
            a_snd[n, j] = fn(q).astype(bf16)
            go(a_copy(n, j))
        for j, q in enumerate((across, w)):
            own[n, j] = fn(q)

    def rs_mid(n):
        a_copy(n, 0).wait_recv()
        b_snd[n] = (own[n, 0] + a_rcv[n, 0].astype(f32)).astype(bf16)
        go(b_copy(n))

    def rs_end(n):
        a_copy(n, 1).wait_recv()
        b_copy(n).wait_recv()
        return own[n, 1] + a_rcv[n, 1].astype(f32) + b_rcv[n].astype(f32)

    def z_copy(n, src, dst, step):
        return remote(
            src, dst, zs_sem.at[n], zr_sem.at[n], {"tm": lax.rem(z + step + tm, tm)}
        )

    def inner_of(i):
        return jnp.logical_and(i > 0, i < tm - 1)

    halo = z_copy(0, sig.at[rows(w)], sj.at[rows(w)], 1)
    go(halo, z < tm - 1)
    sj[seg : 2 * seg] = sig[...]

    @pl.when(z == 0)
    def _():
        sj[0:seg] = jnp.zeros((seg, chans), bf16)
        hj[seg : 2 * seg] = jnp.zeros((seg, chans), bf16)

    @pl.when(z < 2)
    def _():
        hj[0:seg] = jnp.zeros((seg, chans), bf16)

    @pl.loop(0, 4)
    def _(r):
        gg[rows(r), :] = dot_t(cot[rows(r), :], m2[...])

    pl.when(z > 0)(halo.wait_recv)
    sig_gather = Gather(0, sj, 0, z > 0)
    sig_gather.start()
    loads[0].wait()
    loads[1].wait()

    @pl.loop(0, 4)
    def _(r):
        pre[rows(r), :] = dot(sj[rows(r, seg), :], w1[0])

    sig_gather.forward()
    sig_gather.finish()

    def gate(p, a_ref, b_ref, g_ref, q):
        a = jnp.tanh(p[:, :cols])
        b = jax.nn.sigmoid(p[:, cols:])
        a_ref[rows(q), :] = a
        b_ref[rows(q), :] = b
        g = (a * b).astype(bf16)
        g_ref[rows(q), :] = g
        return a, b, g

    def first_quarter(q):
        p = pre[rows(q), :] + dot(sj[rows(q, half_seg), :], w1[1]) + dot(sj[rows(q), :], w1[2])
        g = gate(p, a1, b1, gt1, q)[2]
        return dot(g, m1[...])

    rs_start(0, first_quarter)
    rs_mid(0)
    hj[rows(w, 2 * seg), :] = (sig[rows(w), :].astype(f32) + rs_end(0)).astype(bf16)

    g_own = Gather(1, hj, 2 * seg)
    one = z_copy(1, hj.at[rows(w, 2 * seg)], hj.at[rows(w, seg)], 1)
    two = z_copy(2, hj.at[rows(w, seg)], hj.at[rows(w)], 1)
    g_own.start()
    go(one, z < tm - 1)
    g_own.forward()
    pl.when(z > 0)(one.wait_recv)
    go(two, inner_of(z))
    g_one = Gather(2, hj, seg, z > 0)
    g_one.start()
    g_own.finish()
    loads[2].wait()
    loads[3].wait()

    @pl.loop(0, 4)
    def _(r):
        pre[rows(r), :] = dot(hj[rows(r, 2 * seg), :], w2[0])

    g_one.forward()
    pl.when(z > 1)(two.wait_recv)
    g_two = Gather(3, hj, 0, z > 1)
    g_two.start()
    g_one.finish()

    @pl.loop(0, 4)
    def _(r):
        pre[rows(r), :] += dot(hj[rows(r, seg), :], w2[1])

    g_two.forward()
    g_two.finish()

    def pre_grad(gval, a, b, pg, q):
        pg[rows(q), 0:cols] = (gval * b * (1.0 - a * a)).astype(bf16)
        pg[rows(q), cols : 2 * cols] = (gval * a * b * (1.0 - b)).astype(bf16)

    @pl.loop(0, 4)
    def _(r):
        p = pre[rows(r), :] + dot(hj[rows(r), :], w2[2])
        a, b, _ = gate(p, a2, b2, gt2, r)
        pre_grad(gg[rows(r), :], a, b, pg2, r)

    rs_start(1, lambda q: dot_t(pg2[rows(q), :], w2[2]))
    rs_start(2, lambda q: dot_t(pg2[rows(q), :], w2[1]))
    rs_mid(1)
    rs_start(3, lambda q: dot_t(pg2[rows(q), :], w2[0]))
    rs_mid(2)
    rs_mid(3)

    low = z < 2
    inner = inner_of(z)
    outer = jnp.logical_not(inner)
    far_end = jnp.where(low, tm - 1, 0)
    block_of = (
        far_end,
        jnp.where(low, 2, 1),
        jnp.where(z == 0, 1, jnp.where(z == 1, 0, jnp.where(z == 2, 3, 2))),
        z,
    )
    target_of = (
        jnp.where(z == 0, 1, jnp.where(z == tm - 1, 2, far_end)), block_of[1], block_of[2]
    )
    middle_slot = jnp.where(inner, 2, 3)
    land_of = (0, middle_slot, 1)

    def weight_blocks(n, taps, base, spread, pg, gated, up, slot):
        j = block_of[slot]
        at = pl.ds(pl.multiple_of(j * cblk, cblk), cblk)
        mix = dot_rows(gated[...], up[:, at])
        if slot == 0:
            m_far[n] = mix
        if slot == 3:
            m_own[n] = mix
        else:
            m_snd[n, slot] = mix.astype(bf16)
        for k in range(3):
            lo = base - spread * k
            block = dot_rows(taps[lo : lo + seg, at], pg[...])
            if slot == 0:
                w_far[n, k * cblk : (k + 1) * cblk, :] = block
            if slot == 3:
                w_own[n, k * cblk : (k + 1) * cblk, :] = block
            else:
                w_snd[n, slot, k * cblk : (k + 1) * cblk, :] = block.astype(bf16)

    def w_copies(n, slot, land):
        target = {"tm": target_of[slot]}
        return (
            remote(
                w_snd.at[n, slot], w_rcv.at[n, land], ws_sem.at[n, slot], wr_sem.at[n, land], target
            ),
            remote(
                m_snd.at[n, slot], m_rcv.at[n, land], ms_sem.at[n, slot], mr_sem.at[n, land], target
            ),
        )

    def weight_send(n, slot):
        for copy in w_copies(n, slot, land_of[slot]):
            if slot > 0:
                go(copy)
            else:
                go(copy, outer)

    def weight_relay(n):
        copies = w_copies(n, 0, 0)

        @pl.when(inner)
        def _():
            for copy in copies:
                copy.wait_recv()
            w_snd[n, 0] = (w_far[n] + w_rcv[n, 0].astype(f32)).astype(bf16)
            m_snd[n, 0] = (m_far[n] + m_rcv[n, 0].astype(f32)).astype(bf16)

        for copy in copies:
            go(copy, inner)

    def weight_finish(n, o_f, o_g, o_m):
        def take(land):
            for copy in w_copies(n, 0, land):
                copy.wait_recv()
            w_own[n] += w_rcv[n, land].astype(f32)
            m_own[n] += m_rcv[n, land].astype(f32)

        take(1)

        @pl.when(inner)
        def _():
            take(2)
            take(3)

        @pl.when(outer)
        def _():
            take(0)

        for k in range(3):
            total = w_own[n, k * cblk : (k + 1) * cblk, :] * scale
            o_f[k] = total[:, :cols]
            o_g[k] = total[:, cols:]
        o_m[...] = m_own[n] * scale

    second = (1, hj, 2 * seg, seg, pg2, gt2, cot)
    weight_blocks(*second, 0)
    r_snd[0] = rs_end(1).astype(bf16)
    back_two = z_copy(3, r_snd.at[0], r_rcv.at[0], -1)
    go(back_two, z > 1)
    weight_blocks(*second, 1)
    own[2, 0] = rs_end(2)

    @pl.when(inner_of(z))
    def _():
        back_two.wait_recv()
        own[2, 0] += r_rcv[0].astype(f32)

    r_snd[1] = own[2, 0].astype(bf16)
    back_one = z_copy(4, r_snd.at[1], r_rcv.at[1], -1)
    go(back_one, z > 0)
    weight_send(1, 0)
    weight_send(1, 1)
    weight_blocks(*second, 2)
    weight_send(1, 2)
    own[3, 0] = cot[rows(w), :].astype(f32) + rs_end(3)

    @pl.when(z < tm - 1)
    def _():
        back_one.wait_recv()
        own[3, 0] += r_rcv[1].astype(f32)

    hg[rows(w), :] = own[3, 0].astype(bf16)
    g_hg = Gather(4, hg, 0)
    g_hg.start()
    rs_start(4, lambda q: dot(gt2[rows(q), :], m2[...]))
    g_hg.forward()
    g_hg.finish()

    @pl.loop(0, 4)
    def _(r):
        gval = dot_t(hg[rows(r), :], m1[...])
        pre_grad(gval, a1[rows(r), :], b1[rows(r), :], pg1, r)

    def to_earlier(q):
        late = (q >= 2).astype(f32)
        shifted_q = lax.rem(q + 2, 4)
        return dot_t(pg1[rows(q), :], w1[2]) + late * dot_t(pg1[rows(shifted_q), :], w1[1])

    def to_here(q):
        early = (q < 2).astype(f32)
        shifted_q = lax.rem(q + 2, 4)
        return dot_t(pg1[rows(q), :], w1[0]) + early * dot_t(pg1[rows(shifted_q), :], w1[1])

    rs_start(5, to_earlier)
    first = (0, sj, seg, half_seg, pg1, gt1, hg)
    weight_blocks(*first, 0)
    weight_send(0, 0)
    rs_mid(5)
    rs_start(6, to_here)
    rs_mid(6)
    rs_mid(4)
    weight_blocks(*first, 1)
    r_snd[2] = rs_end(5).astype(bf16)
    back_first = z_copy(5, r_snd.at[2], r_rcv.at[2], -1)
    go(back_first, z > 0)
    weight_send(0, 1)
    weight_relay(1)
    weight_blocks(*first, 2)
    weight_send(0, 2)
    own[6, 0] = hg[rows(w), :].astype(f32) + rs_end(6)

    @pl.when(z < tm - 1)
    def _():
        back_first.wait_recv()
        own[6, 0] += r_rcv[2].astype(f32)

    gxs[rows(w), :] = own[6, 0].astype(bf16)
    g_gx = Gather(5, gxs, 0)
    g_gx.start()
    weight_blocks(*second, 3)
    g_gx.forward()
    weight_blocks(*first, 3)
    o_out2[...] = (hj[rows(w, 2 * seg), :].astype(f32) + rs_end(4)).astype(bf16)
    g_gx.finish()
    o_gx[...] = gxs[...]
    weight_relay(0)
    weight_finish(1, o_cf2, o_cg2, o_mg2)
    weight_finish(0, o_cf1, o_cg1, o_mg1)
    for copy, cond in pending:
        when(cond, copy.wait_send)


def hand_over(*refs):
    for n in range(8):
        refs[8 + n][...] = refs[n][...]


def fused_body(*args):
    sig, cot, f1 = args[:3]
    seg, chans = sig.shape
    cols = f1.shape[2]
    tm = lax.axis_size("tm")
    quarter, cblk = seg // 4, chans // tm
    bf16, f32 = jnp.bfloat16, jnp.float32
    scale = 1.0 / math.sqrt(seg * tm)
    vm = pltpu.VMEM
    dma = pltpu.SemaphoreType.DMA
    wide = 2 * cols
    scratch = [
        vm((2 * seg, chans), bf16),
        vm((3 * seg, chans), bf16),
        vm((3, chans, wide), bf16),
        vm((3, chans, wide), bf16),
        vm((seg, cols), f32),
        vm((seg, cols), f32),
        vm((seg, cols), bf16),
        vm((seg, cols), f32),
        vm((seg, cols), f32),
        vm((seg, cols), bf16),
        vm((seg, cols), f32),
        vm((seg, wide), f32),
        vm((seg, wide), bf16),
        vm((seg, wide), bf16),
        vm((seg, chans), bf16),
        vm((seg, chans), bf16),
        vm((7, 2, quarter, chans), bf16),
        vm((7, 2, quarter, chans), bf16),
        vm((7, quarter, chans), bf16),
        vm((7, quarter, chans), bf16),
        vm((7, 2, quarter, chans), f32),
        vm((3, quarter, chans), bf16),
        vm((3, quarter, chans), bf16),
        vm((2, 3, 3 * cblk, wide), bf16),
        vm((2, 4, 3 * cblk, wide), bf16),
        vm((2, 3 * cblk, wide), f32),
        vm((2, 3 * cblk, wide), f32),
        vm((2, 3, cols, cblk), bf16),
        vm((2, 4, cols, cblk), bf16),
        vm((2, cols, cblk), f32),
        vm((2, cols, cblk), f32),
        dma((4,)),
        dma((7, 2)), dma((7, 2)), dma((7,)), dma((7,)),
        dma((6, 3)), dma((6, 3)),
        dma((6,)), dma((6,)),
        dma((2, 3)), dma((2, 4)), dma((2, 3)), dma((2, 4)),
    ]
    conv = jax.ShapeDtypeStruct((3, cblk, cols), f32)
    mix = jax.ShapeDtypeStruct((cols, cblk), f32)
    in_vm = pl.BlockSpec(memory_space=pltpu.VMEM)
    in_any = pl.BlockSpec(memory_space=pl.ANY)
    shapes = (
        jax.ShapeDtypeStruct((quarter, chans), bf16),
        jax.ShapeDtypeStruct((seg, chans), bf16),
        conv, conv, mix, conv, conv, mix,
    )
    results = pl.pallas_call(
        functools.partial(fused_kernel, tm, scale),
        out_shape=shapes,
        in_specs=[in_vm, in_vm, in_any, in_any, in_vm, in_any, in_any, in_vm],
        out_specs=(in_vm,) * 8,
        scratch_shapes=scratch,
        compiler_params=pltpu.CompilerParams(
            collective_id=0, has_side_effects=True, vmem_limit_bytes=56 * 1024 * 1024
        ),
    )(*args)
    return pl.pallas_call(
        hand_over,
        out_shape=shapes,
        in_specs=[in_vm] * 8,
        out_specs=(in_vm,) * 8,
    )(*results)


def fits(mesh):
    return mesh.shape["wt"] == 4 and mesh.shape["tm"] == 4


def solution(mesh):
    in_specs = (
        P(("grp", "tm"), None),
        P(("grp", "tm"), None),
        P(None, None, "wt"),
        P(None, None, "wt"),
        P("wt", None),
        P(None, None, "wt"),
        P(None, None, "wt"),
        P("wt", None),
    )
    out_specs = (
        P(("grp", "tm", "wt"), None),
        P(("grp", "tm"), None),
        P("grp", "tm", "wt"),
        P("grp", "tm", "wt"),
        P(("grp", "wt"), "tm"),
        P("grp", "tm", "wt"),
        P("grp", "tm", "wt"),
        P(("grp", "wt"), "tm"),
    )
    return jax.shard_map(fused_body if fits(mesh) else body, mesh=mesh, in_specs=in_specs, out_specs=out_specs, check_vma=False)
```
